32 devices in a mesh: row: 2 (over x), col: 4 (over z), rep: 4 (over y, core).
Axes of the slice: x: 2, y: 2, z: 4, core: 2. Of those that a mesh axis runs over, the one named last changes fastest.
Arguments:
- features: bfloat16 [2048, 512], P(('col', 'row'), 'rep'), may hold values from -6 to 6
- weight: bfloat16 [512, 512], replicated, may hold values from -0.25 to 0.25
- tile_pos: int32 [2, 4, 32], P('row', 'col'), may hold values from 0 to 31, as said below
- edges: int32 [2, 4, 32, 64], P('row', 'col'), may hold values from -1 to 16383, as said below
- degree: int32 [2048], P(('row', 'col')), may hold values from 16 to 96
- cotangent: bfloat16 [2048, 512], P(('row', 'col'), 'rep'), may hold values from -6 to 6
Outputs:
- output: bfloat16 [2048, 512], P(('row', 'col'), 'rep')
- grad_weight: float32 [512, 512], P('rep')
- grad_features: bfloat16 [2048, 512], P(('col', 'row'), 'rep')
The draws below stay inside these ranges and needn't reach their ends.
Inputs may be any that keep to these rules, and one draw needn't show every extreme that they name: `tile_pos`: tile places are row tile times CB / 128 plus column tile (RB and CB as in the reference program), distinct within one block. -1 marks an empty slot, any other value is 128 times the target's place in the tile plus the source's place. In each block the live tiles come first and an empty tile holds only -1; within a tile the live slots come first; some block has all 32 tiles live, and every live tile holds 1 to 64 edges.
All inputs are finite; a program needn't handle non-finite values.
Results may differ from the reference program's by a relative error of at most 0.0058.
Values may be sent and summed in bfloat16 or wider, within the bound.
A program may use at most 64 MiB of HBM per device.

```python
import jax
import jax.numpy as jnp
from jax import lax

F_IN = 512
F_OUT = 512
SUB = 256
EPT = 64
TILES = 32
NODES = 2048
N_ROW = 2
N_COL = 4


def draw_tile_pos(key, part):
    key = jax.random.fold_in(key, 7)
    block_total = N_ROW * N_COL
    possible = SUB * N_COL // 128 * (SUB * N_ROW // 128)
    keys = jax.random.split(key, block_total)
    picked = jax.vmap(lambda one_key: jax.random.permutation(one_key, possible)[:TILES])(keys)
    return picked.reshape(N_ROW, N_COL, TILES).astype(jnp.int32)


def draw_edges(key, part):
    key = jax.random.fold_in(key, 11)
    key_live, key_full, key_count, key_tile, key_vals = jax.random.split(key, 5)
    block_total = N_ROW * N_COL
    live = jax.random.randint(key_live, (block_total,), max(1, TILES // 4), TILES + 1)
    full_block = jax.random.randint(key_full, (), 0, block_total)
    live = jnp.where(jnp.arange(block_total) == full_block, TILES, live)
    counts = jax.random.randint(key_count, (block_total, TILES), 1, EPT + 1)
    full_tile = jax.random.randint(key_tile, (block_total,), 0, TILES)
    counts = jnp.where(jnp.arange(TILES)[None, :] == full_tile[:, None], EPT, counts)
    values = jax.random.randint(key_vals, (block_total, TILES, EPT), 0, 16384)
    keep = (jnp.arange(EPT)[None, None, :] < counts[:, :, None]) & (jnp.arange(TILES)[None, :, None] < live[:, None, None])
    return jnp.where(keep, values, -1).reshape(N_ROW, N_COL, TILES, EPT).astype(jnp.int32)


def touch_ends(drawn, own_key, smallest, top_value):
    longest = drawn.shape.index(max(drawn.shape))
    spots = []
    for shift in (0, 1):
        where = [jax.random.randint(jax.random.fold_in(own_key, axis), (), 0, length) for axis, length in enumerate(drawn.shape)]
        where[longest] = (where[longest] + shift) % drawn.shape[longest]
        spots.append(tuple(where))
    return drawn.at[spots[0]].set(smallest).at[spots[1]].set(top_value)


def level_of(rng, shape, pieces, least, largest):
    def one(axis_at, blocks):
        heights = jax.random.uniform(jax.random.fold_in(jax.random.fold_in(rng, 6), axis_at), (blocks,), jnp.float32, least / len(pieces), largest / len(pieces))
        return jnp.repeat(jnp.exp(heights), shape[axis_at] // blocks).reshape((-1,) + (1,) * (len(shape) - axis_at - 1))

    loudness = one(*pieces[0])
    for cut in pieces[1:]:
        loudness = loudness * one(*cut)
    return loudness


def gaussian(key, extent, spread, limit, shards=(), kind=jnp.bfloat16):
    entries = spread * jax.random.normal(key, extent, jnp.float32)
    if shards:
        entries = entries * level_of(key, extent, shards, -0.22, 0.18)
    return jnp.clip(entries, -limit, limit).astype(kind)


def setup_inputs(seed: int = 0) -> dict:
    key_list = jax.random.split(jax.random.key(seed), 7)
    return {
        "features": gaussian(key_list[0], (NODES, F_IN), 1.0, 6.0, ((0, 8), (1, 4))),
        "weight": gaussian(key_list[1], (F_IN, F_OUT), F_IN ** -0.5, 0.25),
        "tile_pos": draw_tile_pos(jax.random.fold_in(key_list[6], 71), 0),
        "edges": draw_edges(jax.random.fold_in(key_list[6], 71), 0),
        "degree": touch_ends(jax.random.randint(key_list[4], (NODES,), 16, 97), jax.random.fold_in(key_list[4], 1), 16, 96).astype(jnp.int32),
        "cotangent": gaussian(key_list[5], (NODES, F_OUT), 1.0, 6.0, ((0, 8), (1, 4))),
    }


def reference(features, weight, tile_pos, edges, degree, cotangent):
    row_span = SUB * N_COL
    col_span = SUB * N_ROW
    col_tiles = col_span // 128
    block_total = N_ROW * N_COL
    places = tile_pos.reshape(block_total, TILES).astype(jnp.int32)
    slots = edges.reshape(block_total, TILES, EPT).astype(jnp.int32)
    block_ids = jnp.arange(block_total, dtype=jnp.int32)

    def endpoints(block_id, place_row, slot_rows):
        row_block = block_id // N_COL
        col_block = block_id % N_COL
        live_mask = slot_rows >= 0
        safe = jnp.where(live_mask, slot_rows, 0)
        targets = row_block * row_span + (place_row // col_tiles)[:, None] * 128 + safe // 128
        sources = col_block * col_span + (place_row % col_tiles)[:, None] * 128 + safe % 128
        return targets.reshape(-1).astype(jnp.int32), sources.reshape(-1).astype(jnp.int32), live_mask.reshape(-1).astype(jnp.float32)

    def forward_step(totals, item):
        targets, sources, live_mask = endpoints(*item)
        rows = features[sources].astype(jnp.float32) * live_mask[:, None]
        return totals.at[targets].add(rows), None

    summed, _ = lax.scan(forward_step, jnp.zeros((NODES, F_IN), jnp.float32), (block_ids, places, slots))
    inverse = 1.0 / degree.astype(jnp.float32)
    agg = (summed * inverse[:, None]).astype(jnp.bfloat16)
    preact = jnp.dot(agg, weight, preferred_element_type=jnp.float32)
    sigmoid_pre = jax.nn.sigmoid(preact)
    output = (preact * sigmoid_pre).astype(jnp.bfloat16)
    silu_slope = sigmoid_pre * (1.0 + preact * (1.0 - sigmoid_pre))
    grad_pre = (cotangent.astype(jnp.float32) * silu_slope).astype(jnp.bfloat16)
    grad_weight = jnp.dot(agg.T, grad_pre, preferred_element_type=jnp.float32)
    grad_agg = jnp.dot(grad_pre, weight.T, preferred_element_type=jnp.float32)
    scaled = (grad_agg * inverse[:, None]).astype(jnp.bfloat16)

    def backward_step(totals, item):
        targets, sources, live_mask = endpoints(*item)
        rows = scaled[targets].astype(jnp.float32) * live_mask[:, None]
        return totals.at[sources].add(rows), None

    back_sum, _ = lax.scan(backward_step, jnp.zeros((NODES, F_IN), jnp.float32), (block_ids, places, slots))
    return output, grad_weight, back_sum.astype(jnp.bfloat16)
```

```python
import functools
import math

import jax
import jax.numpy as jnp
from jax import lax
from jax.experimental import pallas as pl
from jax.experimental.pallas import tpu as pltpu
from jax.sharding import PartitionSpec as P

MESH = pl.DeviceIdType.MESH
BF16 = jnp.bfloat16
F32 = jnp.float32
TILE = 128


def repeat(count, step):
    if count <= 16:
        for index in range(count):
            step(index)
    else:
        lax.fori_loop(0, count, lambda index, carry: (step(index), carry)[1], 0)


def start_of(index, size):
    return index * size if isinstance(index, int) else pl.multiple_of(index * size, size)


def one_hot(values, height):
    ids = lax.broadcasted_iota(jnp.int32, (height, values.shape[1]), 0).astype(F32) + 1.0
    return jnp.where(values == ids, 1.0, 0.0).astype(BF16)


def kernel(
    fused,
    feat_ref, weight_hbm, pos_ref, edges_ref, deg_ref, cot_ref,
    out_ref, gw_ref, gf_ref,
    weight_buf, tsort, ssort, adj, adj_t, xbuf, cot_buf, stage1, recv1,
    agg_buf, aggcol, grad_buf, grad_all, out_stage, stage2, gbuf, stage3, recv3,
    back_own, loc_buf, wstage, wrecv, wall,
    local_sem, s0, r0, sc, rc, s1, r1, so, ro, sa, ra, sg, rg, s2, r2, s3, r3, s4, r4, s5, r5,
):
    rows, cols, reps = lax.axis_size("row"), lax.axis_size("col"), lax.axis_size("rep")
    r, c, p = lax.axis_index("row"), lax.axis_index("col"), lax.axis_index("rep")
    sub, width = feat_ref.shape
    piece = sub // reps
    row_tiles = sub * cols // TILE
    col_tiles = sub * rows // TILE
    edge_slots = edges_ref.shape[3]
    tile_slots = edges_ref.shape[2]

    def turn(at, by, size):
        return lax.rem(at + by, size)

    def back(at, by, size):
        return lax.rem(at + size - by, size)

    load = pltpu.make_async_copy(weight_hbm, weight_buf, local_sem.at[0])
    load.start()

    barrier = pltpu.get_barrier_semaphore()
    plane = [(dc, dp) for dc in range(cols) for dp in range(reps) if dc or dp]
    plane.sort(key=lambda at: -(min(at[0], cols - at[0]) * 4 + min(at[1], reps - at[1])))
    lane = [(dr, dc) for dr in range(rows) for dc in range(cols) if dr or dc]
    greet = [(0, dc, dp) for dc, dp in plane]
    greet += [(dr, dc, 0) for dr, dc in lane if dr and (fused or dc == 0)]
    for dr, dc, dp in greet:
        pl.semaphore_signal(
            barrier, inc=1, device_id=(turn(r, dr, rows), turn(c, dc, cols), turn(p, dp, reps)),
            device_id_type=MESH,
        )

    def push(src, dst, send, recv, to):
        copy = pltpu.make_async_remote_copy(
            src_ref=src, dst_ref=dst, send_sem=send, recv_sem=recv, device_id=to, device_id_type=MESH
        )
        copy.start()
        return copy

    slots = edges_ref[0, 0]
    live = slots >= 0
    targets = jnp.where(live, (slots >> 7) + 1, 0).astype(F32).astype(BF16)
    sources = jnp.where(live, (slots & 127) + 1, 0).astype(F32).astype(BF16)
    places = pos_ref[0]
    group = tsort.shape[2] // edge_slots
    for j in range(col_tiles):
        wanted = lax.broadcasted_iota(jnp.int32, (row_tiles, tile_slots), 0) * col_tiles + j
        pick = jnp.where(wanted == places, 1.0, 0.0).astype(BF16)
        g, k = j // group, j % group
        tsort[g, :, k * edge_slots:(k + 1) * edge_slots] = jnp.dot(
            pick, targets, preferred_element_type=F32
        )
        found = jnp.dot(pick, sources, preferred_element_type=F32)
        ssort[g, :, k * edge_slots:(k + 1) * edge_slots] = jnp.where(found > 0, found + k * 128.0, 0.0)

    pl.semaphore_wait(barrier, len(greet))
    feat_moves = [
        push(
            feat_ref, xbuf.at[pl.ds(pl.multiple_of(r * sub, sub), sub)], s0.at[dr], r0.at[dr],
            (turn(r, dr, rows), c, p),
        )
        for dr in range(1, rows)
    ]
    cot_moves = []
    for dp in range(1, reps):
        q = turn(p, dp, reps)
        cot_moves.append(
            push(
                cot_ref.at[pl.ds(pl.multiple_of(q * piece, piece), piece)], cot_buf.at[p],
                sc.at[dp], rc.at[dp], (r, c, q),
            )
        )
    cot_buf[p] = cot_ref[pl.ds(pl.multiple_of(p * piece, piece), piece)]
    xbuf[pl.ds(pl.multiple_of(r * sub, sub), sub)] = feat_ref[...]

    def build(i):
        at = pl.ds(start_of(i, TILE), TILE)
        for g in range(col_tiles // group):
            span = slice(g * group * TILE, (g + 1) * group * TILE)
            hot_t = one_hot(tsort[g, pl.ds(i, 1), :], TILE)
            hot_s = one_hot(ssort[g, pl.ds(i, 1), :], group * TILE)
            contract = (((1,), (1,)), ((), ()))
            adj[at, span] = lax.dot_general(hot_t, hot_s, contract, preferred_element_type=F32).astype(BF16)
            adj_t[span, at] = lax.dot_general(hot_s, hot_t, contract, preferred_element_type=F32).astype(BF16)

    repeat(row_tiles, build)

    for move in feat_moves:
        move.wait()

    def forward(i):
        at = pl.ds(start_of(i, TILE), TILE)
        stage1[at] = jnp.dot(adj[at], xbuf[...], preferred_element_type=F32).astype(BF16)

    repeat(row_tiles, forward)

    sum_moves = []
    for dc, dp in plane:
        to_c, to_p = turn(c, dc, cols), turn(p, dp, reps)
        first = pl.multiple_of((to_c * reps + to_p) * piece, piece)
        k = dc * reps + dp
        sum_moves.append(
            push(stage1.at[pl.ds(first, piece)], recv1.at[dc, p], s1.at[k], r1.at[k], (r, to_c, to_p))
        )
    recv1[0, p] = stage1[pl.ds(pl.multiple_of((c * reps + p) * piece, piece), piece)]

    ids0 = lax.broadcasted_iota(jnp.int32, (piece, sub), 0)
    ids1 = lax.broadcasted_iota(jnp.int32, (piece, sub), 1)
    degree = jnp.sum(
        jnp.where(ids1 == ids0 + p * piece, deg_ref[...].astype(F32), 0.0), axis=1, keepdims=True
    )
    inverse = 1.0 / degree
    load.wait()
    for move in cot_moves:
        move.wait()
    for move in sum_moves:
        move.wait()

    for q in range(reps):
        total = recv1[0, q].astype(F32)
        for dc in range(1, cols):
            total += recv1[dc, q].astype(F32)
        scaled_sum = (total * inverse).astype(BF16)
        agg_buf[q] = scaled_sum
    agg_moves = []
    for dp in range(1, reps):
        q = turn(p, dp, reps)
        agg_moves.append(push(agg_buf.at[q], aggcol.at[p], sa.at[dp], ra.at[dp], (r, c, q)))
    aggcol[p] = agg_buf[p]

    agg = jnp.concatenate([agg_buf[q] for q in range(reps)], axis=1)
    preact = jnp.dot(agg, weight_buf[...], preferred_element_type=F32)
    sigmoid = jax.nn.sigmoid(preact)
    output = (preact * sigmoid).astype(BF16)
    slope = sigmoid * (1.0 + preact * (1.0 - sigmoid))
    wide = cot_ref.shape[1]
    cot = jnp.concatenate([cot_buf[q] for q in range(reps)], axis=1)
    grad_pre = (cot.astype(F32) * slope).astype(BF16)
    grad_buf[...] = grad_pre
    grad_moves = []
    for dp in range(1, reps):
        q = turn(p, dp, reps)
        grad_moves.append(push(grad_buf, grad_all.at[p], sg.at[dp], rg.at[dp], (r, c, q)))
    grad_all[p] = grad_pre
    grad_agg = lax.dot_general(
        grad_pre, weight_buf[...], (((1,), (1,)), ((), ())), preferred_element_type=F32
    )
    scaled = (grad_agg * inverse).astype(BF16)
    for q in range(reps):
        stage2[q] = scaled[:, q * width:(q + 1) * width]
        out_stage[q] = output[:, q * wide:(q + 1) * wide]
    here = pl.ds(pl.multiple_of((c * reps + p) * piece, piece), piece)
    spread_moves = []
    for dc, dp in plane:
        to_c, to_p = turn(c, dc, cols), turn(p, dp, reps)
        k = dc * reps + dp
        spread_moves.append(push(stage2.at[to_p], gbuf.at[here], s2.at[k], r2.at[k], (r, to_c, to_p)))
    gbuf[here] = stage2[p]
    mine = pl.ds(pl.multiple_of(p * piece, piece), piece)
    out_moves = []
    for dp in range(1, reps):
        q = turn(p, dp, reps)
        out_moves.append(push(out_stage.at[q], out_ref.at[mine], so.at[dp], ro.at[dp], (r, c, q)))
    out_ref[mine] = out_stage[p]

    for move in agg_moves:
        move.wait()
    for move in grad_moves:
        move.wait()
    agg_cols = aggcol[...].reshape(sub, width)
    grad_rows = grad_all[...].reshape(sub, reps * wide)
    local = lax.dot_general(agg_cols, grad_rows, (((0,), (0,)), ((), ())), preferred_element_type=F32)
    if fused:
        part = width // (rows * cols)
        loc_buf[...] = local
        wstage[...] = local.astype(BF16)
        w_moves = []
        for dr, dc in lane:
            to_r, to_c = turn(r, dr, rows), turn(c, dc, cols)
            k = dr * cols + dc
            first = pl.multiple_of((to_r * cols + to_c) * part, part)
            w_moves.append(push(wstage.at[pl.ds(first, part)], wrecv.at[k], s4.at[k], r4.at[k], (to_r, to_c, p)))
    else:
        gw_ref[...] = local

    for move in spread_moves:
        move.wait()
    back_all = jnp.dot(adj_t[...], gbuf[...], preferred_element_type=F32)
    stage3[...] = back_all.astype(BF16)
    back_own[...] = back_all
    back_moves = []
    for dr in range(1, rows):
        to_r = turn(r, dr, rows)
        src = stage3.at[pl.ds(pl.multiple_of(to_r * sub, sub), sub)]
        back_moves.append(push(src, recv3.at[dr], s3.at[dr], r3.at[dr], (to_r, c, p)))

    if fused:
        own = pl.ds(pl.multiple_of((r * cols + c) * part, part), part)
        for move in w_moves:
            move.wait()
        total = loc_buf[own]
        for dr, dc in lane:
            total += wrecv[dr * cols + dc].astype(F32)
        wall[own] = total.astype(BF16)
        all_moves = []
        for dr, dc in lane:
            to_r, to_c = turn(r, dr, rows), turn(c, dc, cols)
            k = dr * cols + dc
            all_moves.append(push(wall.at[own], wall.at[own], s5.at[k], r5.at[k], (to_r, to_c, p)))

    for move in back_moves:
        move.wait()
    total = back_own[pl.ds(pl.multiple_of(r * sub, sub), sub)]
    for dr in range(1, rows):
        total += recv3[dr].astype(F32)
    gf_ref[...] = total.astype(BF16)
    for move in out_moves:
        move.wait()
    if fused:
        for move in all_moves:
            move.wait()
        gw_ref[...] = wall[...].astype(F32)


def body(features, weight, tile_pos, edges, degree, cotangent):
    rows, cols, reps = lax.axis_size("row"), lax.axis_size("col"), lax.axis_size("rep")
    sub, width = features.shape
    wide = cotangent.shape[1]
    piece = sub // reps
    f_in, f_out = weight.shape
    targets, sources = sub * cols, sub * rows
    row_tiles, col_tiles = targets // TILE, sources // TILE
    group = math.gcd(col_tiles, 4)
    fused = width % (rows * cols * 16) == 0
    part = width // (rows * cols) if fused else 16
    lanes = rows * cols if fused else 1
    dma = pltpu.SemaphoreType.DMA
    vmem = pl.BlockSpec(memory_space=pltpu.VMEM)
    scratch = [
        pltpu.VMEM((f_in, f_out), BF16),
        pltpu.VMEM((col_tiles // group, row_tiles, group * edges.shape[3]), F32),
        pltpu.VMEM((col_tiles // group, row_tiles, group * edges.shape[3]), F32),
        pltpu.VMEM((targets, sources), BF16),
        pltpu.VMEM((sources, targets), BF16),
        pltpu.VMEM((sources, width), BF16),
        pltpu.VMEM((reps, piece, wide), BF16),
        pltpu.VMEM((targets, width), BF16),
        pltpu.VMEM((cols, reps, piece, width), BF16),
        pltpu.VMEM((reps, piece, width), BF16),
        pltpu.VMEM((reps, piece, width), BF16),
        pltpu.VMEM((piece, f_out), BF16),
        pltpu.VMEM((reps, piece, f_out), BF16),
        pltpu.VMEM((reps, piece, wide), BF16),
        pltpu.VMEM((reps, piece, width), BF16),
        pltpu.VMEM((targets, width), BF16),
        pltpu.VMEM((sources, width), BF16),
        pltpu.VMEM((rows, sub, width), BF16),
        pltpu.VMEM((sources, width), F32),
        pltpu.VMEM((width, f_out), F32),
        pltpu.VMEM((width, f_out), BF16),
        pltpu.VMEM((lanes, part, f_out), BF16),
        pltpu.VMEM((width, f_out), BF16),
        dma((1,)),
    ]
    for count in (rows, reps, cols * reps, reps, reps, reps, cols * reps, rows, lanes, lanes):
        scratch += [dma((count,)), dma((count,))]
    output, grad_weight, grad_features = pl.pallas_call(
        functools.partial(kernel, fused),
        out_shape=(
            jax.ShapeDtypeStruct((sub, wide), BF16),
            jax.ShapeDtypeStruct((width, f_out), F32),
            jax.ShapeDtypeStruct((sub, width), BF16),
        ),
        in_specs=[vmem, pl.BlockSpec(memory_space=pl.ANY)] + [vmem] * 4,
        out_specs=(vmem, vmem, vmem),
        scratch_shapes=scratch,
        compiler_params=pltpu.CompilerParams(
            collective_id=0, has_side_effects=True, vmem_limit_bytes=52 * 1024 * 1024
        ),
    )(features, weight, tile_pos, edges, degree.reshape(1, sub), cotangent)
    if not fused:
        grad_weight = lax.psum(grad_weight, ("row", "col"))
    return output, grad_weight, grad_features


def solution(mesh):
    placed = (
        P(("col", "row"), "rep"),
        P(),
        P("row", "col", None),
        P("row", "col", None, None),
        P(("row", "col")),
        P(("row", "col"), "rep"),
    )
    return jax.shard_map(
        body,
        mesh=mesh,
        in_specs=placed,
        out_specs=(P(("row", "col"), "rep"), P("rep", None), P(("col", "row"), "rep")),
        check_vma=False,
    )
```

```python
import functools
import math

import jax
import jax.numpy as jnp
from jax import lax
from jax.experimental import pallas as pl
from jax.experimental.pallas import tpu as pltpu
from jax.sharding import PartitionSpec as P

MESH = pl.DeviceIdType.MESH
BF16 = jnp.bfloat16
F32 = jnp.float32
TILE = 128


def repeat(count, step):
    if count <= 16:
        for index in range(count):
            step(index)
    else:
        lax.fori_loop(0, count, lambda index, carry: (step(index), carry)[1], 0)


def start_of(index, size):
    return index * size if isinstance(index, int) else pl.multiple_of(index * size, size)


def one_hot(values, height):
    ids = lax.broadcasted_iota(jnp.int32, (height, values.shape[1]), 0).astype(F32) + 1.0
    return jnp.where(values == ids, 1.0, 0.0).astype(BF16)


def kernel(
    fused,
    feat_hbm, weight_hbm, pos_hbm, edges_hbm, deg_hbm, cot_hbm,
    out_ref, gw_ref, gf_ref,
    feat_ref, weight_buf, weight_t, pos_ref, edges_ref, deg_ref, cot_ref, tsort, ssort, adj, adj_t, xbuf, cot_buf, stage1, recv1,
    agg_buf, aggcol, grad_buf, grad_all, out_stage, stage2, gbuf, stage3, recv3,
    back_own, loc_buf, wstage, wrow, hsum, hstage, wrecv, wall,
    local_sem, s0, r0, sc, rc, s1, r1, so, ro, sa, ra, sg, rg, s2, r2, s3, r3, s4, r4, s5, r5, s6, r6,
):
    rows, cols, reps = lax.axis_size("row"), lax.axis_size("col"), lax.axis_size("rep")
    r, c, p = lax.axis_index("row"), lax.axis_index("col"), lax.axis_index("rep")
    sub, width = feat_ref.shape
    piece = sub // reps
    row_tiles = sub * cols // TILE
    col_tiles = sub * rows // TILE
    edge_slots = edges_ref.shape[3]
    tile_slots = edges_ref.shape[2]

    def turn(at, by, size):
        return lax.rem(at + by, size)

    def back(at, by, size):
        return lax.rem(at + size - by, size)

    pairs = (
        (pos_hbm, pos_ref), (edges_hbm, edges_ref), (feat_hbm, feat_ref),
        (cot_hbm, cot_ref), (deg_hbm, deg_ref), (weight_hbm, weight_buf),
    )
    loads = [pltpu.make_async_copy(src, dst, local_sem.at[k]) for k, (src, dst) in enumerate(pairs)]
    for load in loads:
        load.start()

    barrier = pltpu.get_barrier_semaphore()
    plane = [(dc, dp) for dc in range(cols) for dp in range(reps) if dc or dp]
    plane.sort(key=lambda at: -(min(at[0], cols - at[0]) * 4 + min(at[1], reps - at[1])))
    lane = [(dr, dc) for dr in range(rows) for dc in range(cols) if dr or dc]
    greet = [(0, dc, dp) for dc, dp in plane]
    greet += [(dr, dc, 0) for dr, dc in lane if dr and (fused or dc == 0)]
    for dr, dc, dp in greet:
        pl.semaphore_signal(
            barrier, inc=1, device_id=(turn(r, dr, rows), turn(c, dc, cols), turn(p, dp, reps)),
            device_id_type=MESH,
        )

    def push(src, dst, send, recv, to):
        copy = pltpu.make_async_remote_copy(
            src_ref=src, dst_ref=dst, send_sem=send, recv_sem=recv, device_id=to, device_id_type=MESH
        )
        copy.start()
        return copy

    pl.semaphore_wait(barrier, len(greet))
    feat_moves = [
        push(
            feat_hbm, xbuf.at[pl.ds(pl.multiple_of(r * sub, sub), sub)], s0.at[dr], r0.at[dr],
            (turn(r, dr, rows), c, p),
        )
        for dr in range(1, rows)
    ]
    cot_moves = []
    for dp in range(1, reps):
        q = turn(p, dp, reps)
        cot_moves.append(
            push(
                cot_hbm.at[pl.ds(pl.multiple_of(q * piece, piece), piece)], cot_buf.at[p],
                sc.at[dp], rc.at[dp], (r, c, q),
            )
        )

    loads[0].wait()
    loads[1].wait()
    slots = edges_ref[0, 0]
    live = slots >= 0
    targets = jnp.where(live, (slots >> 7) + 1, 0).astype(F32).astype(BF16)
    sources = jnp.where(live, (slots & 127) + 1, 0).astype(F32).astype(BF16)
    places = pos_ref[0]
    group = tsort.shape[2] // edge_slots
    for j in range(col_tiles):
        wanted = lax.broadcasted_iota(jnp.int32, (row_tiles, tile_slots), 0) * col_tiles + j
        pick = jnp.where(wanted == places, 1.0, 0.0).astype(BF16)
        g, k = j // group, j % group
        tsort[g, :, k * edge_slots:(k + 1) * edge_slots] = jnp.dot(
            pick, targets, preferred_element_type=F32
        )
        found = jnp.dot(pick, sources, preferred_element_type=F32)
        ssort[g, :, k * edge_slots:(k + 1) * edge_slots] = jnp.where(found > 0, found + k * 128.0, 0.0)

    loads[2].wait()
    loads[3].wait()
    cot_buf[p] = cot_ref[pl.ds(pl.multiple_of(p * piece, piece), piece)]
    xbuf[pl.ds(pl.multiple_of(r * sub, sub), sub)] = feat_ref[...]

    def build(i):
        at = pl.ds(start_of(i, TILE), TILE)
        for g in range(col_tiles // group):
            span = slice(g * group * TILE, (g + 1) * group * TILE)
            hot_t = one_hot(tsort[g, pl.ds(i, 1), :], TILE)
            hot_s = one_hot(ssort[g, pl.ds(i, 1), :], group * TILE)
            contract = (((1,), (1,)), ((), ()))
            adj[at, span] = lax.dot_general(hot_t, hot_s, contract, preferred_element_type=F32).astype(BF16)
            adj_t[span, at] = lax.dot_general(hot_s, hot_t, contract, preferred_element_type=F32).astype(BF16)

    repeat(row_tiles, build)

    for move in feat_moves:
        move.wait()

    def forward(i):
        at = pl.ds(start_of(i, TILE), TILE)
        stage1[at] = jnp.dot(adj[at], xbuf[...], preferred_element_type=F32).astype(BF16)

    repeat(row_tiles, forward)

    sum_moves = []
    for dc, dp in plane:
        to_c, to_p = turn(c, dc, cols), turn(p, dp, reps)
        first = pl.multiple_of((to_c * reps + to_p) * piece, piece)
        k = dc * reps + dp
        sum_moves.append(
            push(stage1.at[pl.ds(first, piece)], recv1.at[dc, p], s1.at[k], r1.at[k], (r, to_c, to_p))
        )
    recv1[0, p] = stage1[pl.ds(pl.multiple_of((c * reps + p) * piece, piece), piece)]

    loads[4].wait()
    ids0 = lax.broadcasted_iota(jnp.int32, (piece, sub), 0)
    ids1 = lax.broadcasted_iota(jnp.int32, (piece, sub), 1)
    degree = jnp.sum(
        jnp.where(ids1 == ids0 + p * piece, deg_ref[...].astype(F32), 0.0), axis=1, keepdims=True
    )
    inverse = 1.0 / degree
    loads[5].wait()
    for move in cot_moves:
        move.wait()
    weight_t[...] = weight_buf[...].T
    for move in sum_moves:
        move.wait()

    for q in range(reps):
        total = recv1[0, q].astype(F32)
        for dc in range(1, cols):
            total += recv1[dc, q].astype(F32)
        scaled_sum = (total * inverse).astype(BF16)
        agg_buf[q] = scaled_sum
    agg_moves = []
    for dp in range(1, reps):
        q = turn(p, dp, reps)
        agg_moves.append(push(agg_buf.at[q], aggcol.at[p], sa.at[dp], ra.at[dp], (r, c, q)))
    aggcol[p] = agg_buf[p]

    agg = jnp.concatenate([agg_buf[q] for q in range(reps)], axis=1)
    preact = jnp.dot(agg, weight_buf[...], preferred_element_type=F32)
    sigmoid = jax.nn.sigmoid(preact)
    output = (preact * sigmoid).astype(BF16)
    slope = sigmoid * (1.0 + preact * (1.0 - sigmoid))
    wide = cot_ref.shape[1]
    cot = jnp.concatenate([cot_buf[q] for q in range(reps)], axis=1)
    grad_pre = (cot.astype(F32) * slope).astype(BF16)
    grad_buf[...] = grad_pre
    grad_moves = []
    relay = reps == 4
    beside, across = p + 1 - 2 * lax.rem(p, 2), lax.rem(p + 2, 4)
    if relay:
        far_move = push(grad_buf, grad_all.at[p], sg.at[2], rg.at[2], (r, c, across))
        grad_moves.append(push(grad_buf, grad_all.at[p], sg.at[1], rg.at[1], (r, c, beside)))
    else:
        for dp in range(1, reps):
            q = turn(p, dp, reps)
            grad_moves.append(push(grad_buf, grad_all.at[p], sg.at[dp], rg.at[dp], (r, c, q)))
    grad_all[p] = grad_pre
    grad_agg = jnp.dot(grad_pre, weight_t[...], preferred_element_type=F32)
    scaled = (grad_agg * inverse).astype(BF16)
    for q in range(reps):
        stage2[q] = scaled[:, q * width:(q + 1) * width]
        out_stage[q] = output[:, q * wide:(q + 1) * wide]
    here = pl.ds(pl.multiple_of((c * reps + p) * piece, piece), piece)
    gbuf[here] = stage2[p]
    mine = pl.ds(pl.multiple_of(p * piece, piece), piece)
    if relay:
        far_move.wait()
        grad_moves.append(push(grad_all.at[across], grad_all.at[across], sg.at[3], rg.at[3], (r, c, beside)))
    spread_moves = []
    for dc, dp in plane:
        to_c, to_p = turn(c, dc, cols), turn(p, dp, reps)
        k = dc * reps + dp
        spread_moves.append(push(stage2.at[to_p], gbuf.at[here], s2.at[k], r2.at[k], (r, to_c, to_p)))
    for move in agg_moves:
        move.wait()
    for move in grad_moves:
        move.wait()
    agg_cols = aggcol[...].reshape(sub, width)
    grad_rows = grad_all[...].reshape(sub, reps * wide)
    local = lax.dot_general(agg_cols, grad_rows, (((0,), (0,)), ((), ())), preferred_element_type=F32)
    if fused:
        part = width // (rows * cols)
        half = width // rows
        loc_buf[...] = local
        wstage[...] = local.astype(BF16)
        row_moves = []
        for dr in range(1, rows):
            to_r = turn(r, dr, rows)
            first = pl.multiple_of(to_r * half, half)
            row_moves.append(push(wstage.at[pl.ds(first, half)], wrow.at[dr], s6.at[dr], r6.at[dr], (to_r, c, p)))
        for move in row_moves:
            move.wait()
        total = loc_buf[pl.ds(pl.multiple_of(r * half, half), half)]
        for dr in range(1, rows):
            total += wrow[dr].astype(F32)
        hsum[...] = total
        hstage[...] = total.astype(BF16)
        w_moves = []
        for dc in range(1, cols):
            to_c = turn(c, dc, cols)
            first = pl.multiple_of(to_c * part, part)
            w_moves.append(push(hstage.at[pl.ds(first, part)], wrecv.at[dc], s4.at[dc], r4.at[dc], (r, to_c, p)))
    else:
        gw_ref[...] = local

    out_moves = []
    for dp in range(1, reps):
        q = turn(p, dp, reps)
        out_moves.append(push(out_stage.at[q], out_ref.at[mine], so.at[dp], ro.at[dp], (r, c, q)))
    out_ref[mine] = out_stage[p]

    for move in spread_moves:
        move.wait()
    back_all = jnp.dot(adj_t[...], gbuf[...], preferred_element_type=F32)
    stage3[...] = back_all.astype(BF16)
    back_own[...] = back_all
    back_moves = []
    for dr in range(1, rows):
        to_r = turn(r, dr, rows)
        src = stage3.at[pl.ds(pl.multiple_of(to_r * sub, sub), sub)]
        back_moves.append(push(src, recv3.at[dr], s3.at[dr], r3.at[dr], (to_r, c, p)))

    if fused:
        own = pl.ds(pl.multiple_of((r * cols + c) * part, part), part)
        for move in w_moves:
            move.wait()
        total = hsum[pl.ds(pl.multiple_of(c * part, part), part)]
        for dc in range(1, cols):
            total += wrecv[dc].astype(F32)
        wall[own] = total.astype(BF16)
        all_moves = []
        for dr, dc in lane:
            to_r, to_c = turn(r, dr, rows), turn(c, dc, cols)
            k = dr * cols + dc
            all_moves.append(push(wall.at[own], wall.at[own], s5.at[k], r5.at[k], (to_r, to_c, p)))

    for move in back_moves:
        move.wait()
    total = back_own[pl.ds(pl.multiple_of(r * sub, sub), sub)]
    for dr in range(1, rows):
        total += recv3[dr].astype(F32)
    gf_ref[...] = total.astype(BF16)
    for move in out_moves:
        move.wait()
    if fused:
        for move in all_moves:
            move.wait()
        gw_ref[...] = wall[...].astype(F32)


def store(*refs):
    sems = refs[-1]
    moves = [pltpu.make_async_copy(refs[k], refs[k + 3], sems.at[k]) for k in range(3)]
    for move in moves:
        move.start()
    for move in moves:
        move.wait()


def body(features, weight, tile_pos, edges, degree, cotangent):
    rows, cols, reps = lax.axis_size("row"), lax.axis_size("col"), lax.axis_size("rep")
    sub, width = features.shape
    wide = cotangent.shape[1]
    piece = sub // reps
    f_in, f_out = weight.shape
    targets, sources = sub * cols, sub * rows
    row_tiles, col_tiles = targets // TILE, sources // TILE
    group = math.gcd(col_tiles, 4)
    fused = width % (rows * cols * 16) == 0
    part = width // (rows * cols) if fused else 16
    lanes = rows * cols if fused else 1
    half = part * cols if fused else 16
    dma = pltpu.SemaphoreType.DMA
    grant = 61 * 1024 * 1024
    vmem = pl.BlockSpec(memory_space=pltpu.VMEM)
    hbm = pl.BlockSpec(memory_space=pltpu.HBM)
    scratch = [
        pltpu.VMEM(features.shape, BF16),
        pltpu.VMEM((f_in, f_out), BF16),
        pltpu.VMEM((f_out, f_in), BF16),
        pltpu.VMEM(tile_pos.shape, jnp.int32),
        pltpu.VMEM(edges.shape, jnp.int32),
        pltpu.VMEM((1, sub), jnp.int32),
        pltpu.VMEM(cotangent.shape, BF16),
        pltpu.VMEM((col_tiles // group, row_tiles, group * edges.shape[3]), F32),
        pltpu.VMEM((col_tiles // group, row_tiles, group * edges.shape[3]), F32),
        pltpu.VMEM((targets, sources), BF16),
        pltpu.VMEM((sources, targets), BF16),
        pltpu.VMEM((sources, width), BF16),
        pltpu.VMEM((reps, piece, wide), BF16),
        pltpu.VMEM((targets, width), BF16),
        pltpu.VMEM((cols, reps, piece, width), BF16),
        pltpu.VMEM((reps, piece, width), BF16),
        pltpu.VMEM((reps, piece, width), BF16),
        pltpu.VMEM((piece, f_out), BF16),
        pltpu.VMEM((reps, piece, f_out), BF16),
        pltpu.VMEM((reps, piece, wide), BF16),
        pltpu.VMEM((reps, piece, width), BF16),
        pltpu.VMEM((targets, width), BF16),
        pltpu.VMEM((sources, width), BF16),
        pltpu.VMEM((rows, sub, width), BF16),
        pltpu.VMEM((sources, width), F32),
        pltpu.VMEM((width, f_out), F32),
        pltpu.VMEM((width, f_out), BF16),
        pltpu.VMEM((rows if fused else 1, half, f_out), BF16),
        pltpu.VMEM((half, f_out), F32),
        pltpu.VMEM((half, f_out), BF16),
        pltpu.VMEM((cols, part, f_out), BF16),
        pltpu.VMEM((width, f_out), BF16),
        dma((6,)),
    ]
    for count in (rows, reps, cols * reps, reps, reps, reps, cols * reps, rows, cols, lanes, rows):
        scratch += [dma((count,)), dma((count,))]
    output, grad_weight, grad_features = pl.pallas_call(
        functools.partial(kernel, fused),
        out_shape=(
            jax.ShapeDtypeStruct((sub, wide), BF16),
            jax.ShapeDtypeStruct((width, f_out), F32),
            jax.ShapeDtypeStruct((sub, width), BF16),
        ),
        in_specs=[hbm] * 6,
        out_specs=(vmem,) * 3,
        scratch_shapes=scratch,
        compiler_params=pltpu.CompilerParams(
            collective_id=0, has_side_effects=True, vmem_limit_bytes=grant
        ),
    )(features, weight, tile_pos, edges, degree.reshape(1, sub), cotangent)
    if not fused:
        grad_weight = lax.psum(grad_weight, ("row", "col"))
    results = (output, grad_weight, grad_features)
    return pl.pallas_call(
        store,
        out_shape=tuple(jax.ShapeDtypeStruct(result.shape, result.dtype) for result in results),
        in_specs=[vmem] * 3,
        out_specs=(hbm,) * 3,
        scratch_shapes=[dma((3,))],
        compiler_params=pltpu.CompilerParams(vmem_limit_bytes=grant),
    )(*results)


def solution(mesh):
    placed = (
        P(("col", "row"), "rep"),
        P(),
        P("row", "col", None),
        P("row", "col", None, None),
        P(("row", "col")),
        P(("row", "col"), "rep"),
    )
    return jax.shard_map(
        body,
        mesh=mesh,
        in_specs=placed,
        out_specs=(P(("row", "col"), "rep"), P("rep", None), P(("col", "row"), "rep")),
        check_vma=False,
    )
```
